256 devices in a mesh: rows: 16 (over z, x_lo), cols: 16 (over x_hi, y, core).
Axes of the slice: x: 4 (x_hi: 2, x_lo: 2; x = x_hi * 2 + x_lo), y: 4, z: 8, core: 2. Of those that a mesh axis runs over, the one named last changes fastest.
Arguments:
- columns: bfloat16 [16384, 8192], P('rows', 'cols'), may hold values from -30 to 30
- column_order: int32 [512], replicated, may hold values from 0 to 511, each once
- section_bits: int32 [3], replicated, may hold values from 0 to 3, as said below
Outputs:
- rotated: float32 [16384, 8192], P('rows', 'cols')
The draws below stay inside these ranges and needn't reach their ends.
Inputs may be any that keep to these rules, and one draw needn't show every extreme that they name: `section_bits`: bit numbers of a column pair index, repeats allowed; bit 0 and the highest bit are always among them.
All inputs are finite; a program needn't handle non-finite values.
Results may differ from the reference program's by a relative error of at most 0.0046.
Values may be sent and summed in bfloat16 or wider, within the bound.
A program may use at most 64 MiB of HBM per device.

```python
import math
import jax
import jax.numpy as jnp
from jax import lax

BLK = 256
SECTIONS = 3
ITERS = 4
ROWS = 16384
NCOL = 8192
N_COLS = 16


def draw_columns(key, part):
    key = jax.random.fold_in(key, 11)
    key_rows, key_cols, key_base = jax.random.split(key, 3)
    position = jnp.arange(ROWS, dtype=jnp.float32) / ROWS
    row_scale = jnp.exp(jax.random.uniform(key_rows, (ROWS, 1), minval=0.0, maxval=math.log(10.0)) + math.log(3.0) * position[:, None])
    col_scale = jnp.exp(jax.random.uniform(key_cols, (1, NCOL), minval=0.0, maxval=math.log(10.0)))
    base = jax.random.normal(key_base, (ROWS, NCOL))
    base = jnp.clip(base, -5.0, 5.0)
    return (0.02 * base * row_scale * col_scale).astype(jnp.bfloat16)


def draw_section_bits(key, part):
    key = jax.random.fold_in(key, 23)
    key_extra, key_order = jax.random.split(key, 2)
    bit_count = int(N_COLS).bit_length() - 1
    ends = jnp.array([0, bit_count - 1], dtype=jnp.int32)
    extra = jax.random.randint(key_extra, (SECTIONS - 2,), 0, bit_count).astype(jnp.int32)
    chosen = jnp.concatenate([ends, extra])
    return jax.random.permutation(key_order, chosen).astype(jnp.int32)


def setup_inputs(seed: int = 0) -> dict:
    key_of = jax.random.split(jax.random.key(seed), 4)
    return {
        "columns": draw_columns(jax.random.fold_in(key_of[3], 71), 0),
        "column_order": jax.random.permutation(key_of[1], 2 * BLK).astype(jnp.int32),
        "section_bits": draw_section_bits(jax.random.fold_in(key_of[3], 71), 0),
    }


EPS = 1e-06
THETA = 4.0
HIGH = lax.Precision.HIGHEST

def rotation(gram_matrix):
    pair_width = gram_matrix.shape[0]
    ramp_values = jnp.arange(pair_width, dtype=jnp.float32) / pair_width
    root_values = jnp.sqrt(jnp.diagonal(gram_matrix) + EPS)
    scaled_gram = gram_matrix / (root_values[:, None] * root_values[None, :])
    commutator = THETA * (ramp_values[:, None] - ramp_values[None, :]) * scaled_gram
    frobenius = jnp.sum(commutator * commutator)
    iterate = (jnp.eye(pair_width, dtype=jnp.float32) + commutator) / jnp.sqrt(1.0 + frobenius)
    for sweep_index in range(ITERS):
        product = lax.dot_general(iterate, iterate, (((0,), (0,)), ((), ())), precision=HIGH, preferred_element_type=jnp.float32)
        iterate = 1.5 * iterate - 0.5 * jnp.dot(iterate, product, precision=HIGH, preferred_element_type=jnp.float32)
    return iterate

def apply_rotation(column_pair):
    gram_matrix = lax.dot_general(column_pair, column_pair, (((0,), (0,)), ((), ())), preferred_element_type=jnp.float32)
    rotation_matrix = rotation(gram_matrix)
    return jnp.dot(column_pair.astype(jnp.float32), rotation_matrix, precision=HIGH, preferred_element_type=jnp.float32)

def reference(columns, column_order, section_bits):
    all_pairs = columns.reshape(ROWS, N_COLS, 2 * BLK)
    all_pairs = jnp.take(all_pairs, column_order.astype(jnp.int32), axis=2)
    pair_index = jnp.arange(N_COLS, dtype=jnp.int32)
    result = None
    for section_index in range(SECTIONS):
        shifted = jnp.left_shift(jnp.ones((), jnp.int32), section_bits[section_index].astype(jnp.int32))
        partner_index = jnp.bitwise_xor(pair_index, shifted)
        incoming = jnp.take(all_pairs[:, :, BLK:], partner_index, axis=1)
        all_pairs = jnp.concatenate([all_pairs[:, :, :BLK], incoming], axis=2)
        rotated_pairs = jnp.moveaxis(lax.map(apply_rotation, jnp.moveaxis(all_pairs, 1, 0)), 0, 1)
        if section_index + 1 < SECTIONS:
            all_pairs = rotated_pairs.astype(jnp.bfloat16)
        else:
            result = rotated_pairs
    return result.reshape(ROWS, N_COLS * 2 * BLK)
```

```python
import functools

import jax
import jax.numpy as jnp
from jax import lax
from jax.experimental import pallas as pl
from jax.experimental.pallas import tpu as pltpu
from jax.sharding import PartitionSpec as P

SECTIONS = 3
ITERS = 4
EPS = 1e-06
THETA = 4.0
MESH = pl.DeviceIdType.MESH
BF = jnp.bfloat16
F32 = jnp.float32
TILE = 256


def dot(a, b):
    return jnp.dot(a, b, preferred_element_type=F32)


def dot_tn(a, b):
    return lax.dot_general(a, b, (((0,), (0,)), ((), ())), preferred_element_type=F32)


def dot_nt(a, b):
    return lax.dot_general(a, b, (((1,), (1,)), ((), ())), preferred_element_type=F32)


def split(a):
    high = a.astype(BF)
    return high, (a - high.astype(F32)).astype(BF)


def packed(block):
    half = block.shape[0] // 2
    return jnp.concatenate([block[:half, :], block[half:, half:]], axis=1)


def unpacked(block):
    half = block.shape[0]
    a, b, d = block[:, :half], block[:, half : 2 * half], block[:, 2 * half :]
    return jnp.concatenate(
        [jnp.concatenate([a, b], axis=1), jnp.concatenate([b.T, d], axis=1)], axis=0
    )


def rotation(kk, km, mm):
    width = kk.shape[0]
    total = 2 * width
    row = lax.broadcasted_iota(jnp.int32, (width, width), 0)
    col = lax.broadcasted_iota(jnp.int32, (width, width), 1)
    eye = row == col
    gap = (row - col).astype(F32) * (THETA / total)

    def inverse_roots(block, axis):
        d = jnp.sum(jnp.where(eye, block, 0.0), axis=axis, keepdims=True)
        return 1.0 / jnp.sqrt(d + EPS)

    k_col, k_row = inverse_roots(kk, 1), inverse_roots(kk, 0)
    m_col, m_row = inverse_roots(mm, 1), inverse_roots(mm, 0)
    c_kk = gap * (kk * (k_col * k_row))
    c_mm = gap * (mm * (m_col * m_row))
    c_km = (gap - THETA * 0.5) * (km * (k_col * m_row))
    frob = jnp.sum(c_kk * c_kk) + 2.0 * jnp.sum(c_km * c_km) + jnp.sum(c_mm * c_mm)
    z = jnp.concatenate(
        [jnp.concatenate([c_kk, c_km], axis=1), jnp.concatenate([-c_km.T, c_mm], axis=1)],
        axis=0,
    )
    scale = 1.0 / jnp.sqrt(jnp.full((1, 1), 1.0, F32) + frob)
    for k in range(ITERS):
        zb = z.astype(BF)
        w = dot_nt(zb, zb)
        if k:
            w = w + (z + z.T)
        square = scale * scale
        b = 1.5 - 0.5 * square
        z = z - (0.5 * square / b) * (w + dot(zb, w.astype(BF)))
        scale = scale * b
    row = lax.broadcasted_iota(jnp.int32, (total, total), 0)
    col = lax.broadcasted_iota(jnp.int32, (total, total), 1)
    return scale * (z + jnp.where(row == col, 1.0, 0.0))


def meet_kernel(bit, kind, p_ref, high_ref, *rest):
    low_ref, rest = (rest[0], rest[1:]) if kind == BF else (None, rest)
    new_ref, pair_ref, gram_a, gram_b, part_a, landed_a, handed, part_b, landed_b, g_ref, swap_sems, sums, hands = rest
    group = lax.axis_size("rows")
    ring = group // 2
    me_r, me_c = lax.axis_index("rows"), lax.axis_index("cols")
    me_z, me_x = me_r // 2, me_r % 2
    rows, total = p_ref.shape
    half = total // 2
    quarter = half // 2
    tiles = rows // TILE
    rows_each = quarter // group
    partner = me_c + (1 << bit) * (1 - 2 * ((me_c // (1 << bit)) % 2))
    sems_a, sems_b = sums.at[0], sums.at[1]
    kk_ref, km_ref, mm_ref = g_ref.at[0], g_ref.at[1], g_ref.at[2]

    def each_peer(act):
        def visit(i, carry):
            k = i // 2
            z = ring // 2 + ((k + 1) // 2) * (1 - 2 * (k % 2))
            act(((me_z + z) % ring) * 2 + (me_x + 1 + i) % 2)
            return carry

        lax.fori_loop(0, group - 1, visit, 0)

    def to(device, source, target, send_sem, recv_sem):
        return pltpu.make_async_remote_copy(
            src_ref=source,
            dst_ref=target,
            send_sem=send_sem,
            recv_sem=recv_sem,
            device_id=device,
            device_id_type=MESH,
        )

    def rows_of(t):
        return pl.ds(pl.multiple_of(t * TILE, TILE), TILE)

    def swap(t):
        return to(
            (me_r, partner),
            new_ref.at[rows_of(t), :],
            pair_ref.at[rows_of(t), half:],
            swap_sems.at[0, t],
            swap_sems.at[1, t],
        )

    def wait_all(buffer, sem):
        others = buffer.at[pl.ds(0, group - 1)]
        pltpu.make_async_copy(others, others, sem).wait()

    def start_sum(part, landed, sems):
        each_peer(
            lambda peer: to(
                (peer, me_c), part.at[peer], landed.at[me_r], sems.at[0], sems.at[1]
            ).start()
        )
        landed[me_r] = part[me_r]

    def end_sum(landed, sems):
        wait_all(landed, sems.at[1])
        out = landed[0].astype(F32)
        for k in range(1, group):
            out += landed[k].astype(F32)
        return out

    def start_gather(gram, sems):
        each_peer(
            lambda peer: to(
                (peer, me_c), gram.at[me_r], gram.at[me_r], sems.at[2], sems.at[3]
            ).start()
        )

    barrier = pltpu.get_barrier_semaphore()
    each_peer(
        lambda peer: pl.semaphore_signal(
            barrier, inc=1, device_id=(peer, me_c), device_id_type=MESH
        )
    )
    pl.semaphore_signal(barrier, inc=1, device_id=(me_r, partner), device_id_type=MESH)

    g_ref[...] = jnp.zeros_like(g_ref)

    def turn_kept(t, carry):
        old = p_ref[rows_of(t), :]
        new = dot(old, high_ref[...])
        if low_ref is not None:
            new += dot(old, low_ref[...])
        new = new.astype(BF)
        pair_ref[rows_of(t), :half] = new
        kk_ref[...] += dot_tn(new, new)
        return carry

    lax.fori_loop(0, tiles, turn_kept, 0)
    pl.semaphore_wait(barrier, group)

    def leave(t, carry):
        swap(t).start()
        return carry

    lax.fori_loop(0, tiles, leave, 0)

    def square(t, carry):
        old = new_ref[rows_of(t), :]
        mm_ref[...] += dot_tn(old, old)
        return carry

    lax.fori_loop(0, tiles, square, 0)
    shape = (group, rows_each, half + quarter)
    part_a[...] = jnp.concatenate(
        [packed(kk_ref[...]).reshape(shape), packed(mm_ref[...]).reshape(shape)], axis=1
    ).astype(kind)
    start_sum(part_a, landed_a, sems_a)

    def cross(t, carry):
        swap(t).wait()
        km_ref[...] += dot_tn(pair_ref[rows_of(t), :half], pair_ref[rows_of(t), half:])
        return carry

    lax.fori_loop(0, tiles - 1, cross, 0)
    if bit == 0:
        lax.fori_loop(tiles - 1, tiles, cross, 0)
        part_b[...] = km_ref[...].reshape(group, half // group, half).astype(kind)
        start_sum(part_b, landed_b, sems_b)
    mine = end_sum(landed_a, sems_a)
    gram_a[me_r] = mine.astype(kind)
    hand = to((me_r, partner), gram_a.at[me_r], handed, hands.at[0], hands.at[1])
    hand.start()
    if bit:
        lax.fori_loop(tiles - 1, tiles, cross, 0)
        part_b[...] = km_ref[...].reshape(group, half // group, half).astype(kind)
        start_sum(part_b, landed_b, sems_b)
    hand.wait()
    place = lax.broadcasted_iota(jnp.int32, mine.shape, 0)
    gram_a[me_r] = jnp.where(place < rows_each, mine, handed[...].astype(F32)).astype(kind)
    start_gather(gram_a, sems_a)
    gram_b[me_r] = end_sum(landed_b, sems_b).astype(kind)
    start_gather(gram_b, sems_b)
    wait_all(part_a, sems_a.at[0])
    wait_all(part_b, sems_b.at[0])
    wait_all(gram_a, sems_a.at[3])
    wait_all(gram_b, sems_b.at[3])
    wait_all(gram_a, sems_a.at[2])
    wait_all(gram_b, sems_b.at[2])


def meet(p, *rest, bit, kind, site):
    rows, total = p.shape
    half, quarter = total // 2, total // 4
    group = lax.axis_size("rows")
    chunk = half // group
    side = (group, chunk, half + quarter)
    full = (group, chunk, half)
    vmem = pl.BlockSpec(memory_space=pltpu.VMEM)
    return pl.pallas_call(
        functools.partial(meet_kernel, bit, kind),
        out_shape=(
            jax.ShapeDtypeStruct((rows, total), BF),
            jax.ShapeDtypeStruct(side, kind),
            jax.ShapeDtypeStruct(full, kind),
        ),
        in_specs=[vmem] * (1 + len(rest)),
        out_specs=[vmem] * 3,
        scratch_shapes=[
            pltpu.VMEM(side, kind),
            pltpu.VMEM(side, kind),
            pltpu.VMEM(side[1:], kind),
            pltpu.VMEM(full, kind),
            pltpu.VMEM(full, kind),
            pltpu.VMEM((3, half, half), F32),
            pltpu.SemaphoreType.DMA((2, rows // TILE)),
            pltpu.SemaphoreType.DMA((2, 4)),
            pltpu.SemaphoreType.DMA((2,)),
        ],
        compiler_params=pltpu.CompilerParams(
            collective_id=site, has_side_effects=True, vmem_limit_bytes=48 << 20
        ),
        name=f"meet_bit{bit}",
    )(p, *rest)


def start_kernel(p_ref, order_ref, high_ref, new_ref):
    rows, total = p_ref.shape
    half = total // 2
    old = lax.broadcasted_iota(jnp.int32, (total, total), 0)
    pick = jnp.where(old == order_ref[...], 1.0, 0.0).astype(BF)
    high_ref[...] = pick[:, :half]
    for t in range(0, rows, TILE):
        new_ref[t : t + TILE, :] = dot(p_ref[t : t + TILE, :], pick[:, half:]).astype(BF)


def start(p, order):
    rows, total = p.shape
    half = total // 2
    return pl.pallas_call(
        start_kernel,
        out_shape=(
            jax.ShapeDtypeStruct((total, half), BF),
            jax.ShapeDtypeStruct((rows, half), BF),
        ),
        compiler_params=pltpu.CompilerParams(vmem_limit_bytes=48 << 20),
        name="start",
    )(p, order)


def turn_kernel(last, p_ref, gram_a, gram_b, *outs):
    rows, total = p_ref.shape
    half = total // 2
    quarter = half // 2
    group = gram_a.shape[0]
    each = quarter // group
    g = gram_a[...].astype(F32)
    kk = unpacked(g[:, :each, :].reshape(quarter, -1))
    mm = unpacked(g[:, each:, :].reshape(quarter, -1))
    high, low = split(rotation(kk, gram_b[...].astype(F32).reshape(half, half), mm))
    if not last:
        high_ref, low_ref, new_ref = outs
        high_ref[...], low_ref[...] = high[:, :half], low[:, :half]
        high, low = high[:, half:], low[:, half:]
    for t in range(0, rows, TILE):
        tile = p_ref[t : t + TILE, :]
        out = dot(tile, high) + dot(tile, low)
        if last:
            outs[0][t : t + TILE, :] = out
        else:
            new_ref[t : t + TILE, :] = out.astype(BF)


def turn(p, gram_a, gram_b, last):
    rows, total = p.shape
    half = total // 2
    out_shape = [jax.ShapeDtypeStruct((rows, total), F32)]
    if not last:
        out_shape = [jax.ShapeDtypeStruct((total, half), BF)] * 2
        out_shape += [jax.ShapeDtypeStruct((rows, half), BF)]
    return pl.pallas_call(
        functools.partial(turn_kernel, last),
        out_shape=out_shape,
        compiler_params=pltpu.CompilerParams(vmem_limit_bytes=48 << 20),
        name="last_turn" if last else "turn",
    )(p, gram_a, gram_b)


def shards(columns, column_order, section_bits):
    levels = lax.axis_size("cols").bit_length() - 1
    p, rest = columns, start(columns, column_order.reshape(1, -1))
    for s in range(SECTIONS):
        branches = [
            functools.partial(meet, bit=bit, kind=BF if s else F32, site=s * levels + bit)
            for bit in range(levels)
        ]
        p, gram_a, gram_b = lax.switch(section_bits[s], branches, p, *rest)
        rest = turn(p, gram_a, gram_b, s + 1 == SECTIONS)
    return rest[0]


def solution(mesh):
    return jax.shard_map(
        shards,
        mesh=mesh,
        in_specs=(P("rows", "cols"), P(), P()),
        out_specs=P("rows", "cols"),
        check_vma=False,
    )
```

```python
import functools

import jax
import jax.numpy as jnp
from jax import lax
from jax.experimental import pallas as pl
from jax.experimental.pallas import tpu as pltpu
from jax.sharding import PartitionSpec as P

SECTIONS = 3
ITERS = 4
EPS = 1e-06
THETA = 4.0
MESH = pl.DeviceIdType.MESH
BF = jnp.bfloat16
F32 = jnp.float32
TILE = 256


def dot(a, b):
    return jnp.dot(a, b, preferred_element_type=F32)


def dot_tn(a, b):
    return lax.dot_general(a, b, (((0,), (0,)), ((), ())), preferred_element_type=F32)


def dot_nt(a, b):
    return lax.dot_general(a, b, (((1,), (1,)), ((), ())), preferred_element_type=F32)


def split(a):
    high = a.astype(BF)
    return high, (a - high.astype(F32)).astype(BF)


def packed(block):
    half = block.shape[0] // 2
    return jnp.concatenate([block[:half, :], block[half:, half:]], axis=1)


def unpacked(block):
    half = block.shape[0]
    a, b, d = block[:, :half], block[:, half : 2 * half], block[:, 2 * half :]
    return jnp.concatenate(
        [jnp.concatenate([a, b], axis=1), jnp.concatenate([b.T, d], axis=1)], axis=0
    )


def rotation(kk, km, mm):
    width = kk.shape[0]
    total = 2 * width
    row = lax.broadcasted_iota(jnp.int32, (width, width), 0)
    col = lax.broadcasted_iota(jnp.int32, (width, width), 1)
    eye = row == col
    gap = (row - col).astype(F32) * (THETA / total)

    def inverse_roots(block, axis):
        d = jnp.sum(jnp.where(eye, block, 0.0), axis=axis, keepdims=True)
        return 1.0 / jnp.sqrt(d + EPS)

    k_col, k_row = inverse_roots(kk, 1), inverse_roots(kk, 0)
    m_col, m_row = inverse_roots(mm, 1), inverse_roots(mm, 0)
    c_kk = gap * (kk * (k_col * k_row))
    c_mm = gap * (mm * (m_col * m_row))
    c_km = (gap - THETA * 0.5) * (km * (k_col * m_row))
    frob = jnp.sum(c_kk * c_kk) + 2.0 * jnp.sum(c_km * c_km) + jnp.sum(c_mm * c_mm)
    z = jnp.concatenate(
        [jnp.concatenate([c_kk, c_km], axis=1), jnp.concatenate([-c_km.T, c_mm], axis=1)],
        axis=0,
    )
    scale = 1.0 / jnp.sqrt(jnp.full((1, 1), 1.0, F32) + frob)
    for k in range(ITERS):
        zb = z.astype(BF)
        w = dot_nt(zb, zb)
        if k:
            w = w + (z + z.T)
        square = scale * scale
        b = 1.5 - 0.5 * square
        z = z - (0.5 * square / b) * (w + dot(zb, w.astype(BF)))
        scale = scale * b
    row = lax.broadcasted_iota(jnp.int32, (total, total), 0)
    col = lax.broadcasted_iota(jnp.int32, (total, total), 1)
    return scale * (z + jnp.where(row == col, 1.0, 0.0))


def meet_kernel(bit, first, p_ref, *rest):
    if first:
        order_hbm, pair_ref, gram_a, gram_b, old_ref, moving, order_ref, high_ref, load_sems, *rest = rest
        low_ref = None
    else:
        high_ref, low_ref, moving, pair_ref, gram_a, gram_b, *rest = rest
        old_ref = p_ref
    part_a, landed_a, handed, part_b, landed_b, g_ref, swap_sems, sums, hands = rest
    kind = part_b.dtype
    kk_ref, km_ref, mm_ref = g_ref.at[0], g_ref.at[1], g_ref.at[2]
    group = lax.axis_size("rows")
    ring = group // 2
    me_r, me_c = lax.axis_index("rows"), lax.axis_index("cols")
    me_z, me_x = me_r // 2, me_r % 2
    rows, total = p_ref.shape
    half = total // 2
    quarter = half // 2
    tiles = rows // TILE
    rows_each = quarter // group
    partner = me_c + (1 << bit) * (1 - 2 * ((me_c // (1 << bit)) % 2))
    sems_a, sems_b = sums.at[0], sums.at[1]

    def each_peer(act):
        def visit(i, carry):
            k = i // 2
            z = ring // 2 + ((k + 1) // 2) * (1 - 2 * (k % 2))
            act(((me_z + z) % ring) * 2 + (me_x + 1 + i) % 2)
            return carry

        lax.fori_loop(0, group - 1, visit, 0)

    def to(device, source, target, send_sem, recv_sem):
        return pltpu.make_async_remote_copy(
            src_ref=source,
            dst_ref=target,
            send_sem=send_sem,
            recv_sem=recv_sem,
            device_id=device,
            device_id_type=MESH,
        )

    def rows_of(t):
        return pl.ds(pl.multiple_of(t * TILE, TILE), TILE)

    def swap(t):
        return to(
            (me_r, partner),
            moving.at[rows_of(t), :],
            pair_ref.at[rows_of(t), half:],
            swap_sems.at[0, t],
            swap_sems.at[1, t],
        )

    def wait_all(buffer, sem):
        others = buffer.at[pl.ds(0, group - 1)]
        pltpu.make_async_copy(others, others, sem).wait()

    def start_sum(part, landed, sems):
        each_peer(
            lambda peer: to(
                (peer, me_c), part.at[peer], landed.at[me_r], sems.at[0], sems.at[1]
            ).start()
        )
        landed[me_r] = part[me_r]

    def end_sum(landed, sems):
        wait_all(landed, sems.at[1])
        out = landed[0].astype(F32)
        for k in range(1, group):
            out += landed[k].astype(F32)
        return out

    def start_gather(gram, sems):
        each_peer(
            lambda peer: to(
                (peer, me_c), gram.at[me_r], gram.at[me_r], sems.at[2], sems.at[3]
            ).start()
        )

    def with_low_diagonals(block):
        high, low = split(block)
        row = lax.broadcasted_iota(jnp.int32, block.shape, 0) % rows_each + me_r * rows_each
        col = lax.broadcasted_iota(jnp.int32, block.shape, 1)
        low = low.astype(F32)
        first_low = jnp.sum(jnp.where(col == row, low, 0.0), axis=1, keepdims=True)
        last_low = jnp.sum(jnp.where(col == row + half, low, 0.0), axis=1, keepdims=True)
        lane = lax.broadcasted_iota(jnp.int32, (block.shape[0], quarter), 1)
        lows = jnp.where(lane == 0, first_low, jnp.where(lane == 1, last_low, 0.0))
        return jnp.concatenate([high, lows.astype(BF)], axis=1)

    barrier = pltpu.get_barrier_semaphore()
    each_peer(
        lambda peer: pl.semaphore_signal(
            barrier, inc=1, device_id=(peer, me_c), device_id_type=MESH
        )
    )
    pl.semaphore_signal(barrier, inc=1, device_id=(me_r, partner), device_id_type=MESH)

    g_ref[...] = jnp.zeros_like(g_ref)
    if first:
        load = pltpu.make_async_copy(p_ref, old_ref, load_sems.at[0])
        load.start()
        load_order = pltpu.make_async_copy(order_hbm, order_ref, load_sems.at[1])
        load_order.start()
        load_order.wait()
        old_place = lax.broadcasted_iota(jnp.int32, (total, total), 0)
        high_ref[...] = jnp.where(old_place == order_ref[...], 1.0, 0.0).astype(BF)
        load.wait()

        def order_moving(t, carry):
            moving[rows_of(t), :] = dot(old_ref[rows_of(t), :], high_ref[:, half:]).astype(BF)
            return carry

        lax.fori_loop(0, tiles, order_moving, 0)

    def turn_kept(t, carry):
        old = old_ref[rows_of(t), :]
        new = dot(old, high_ref[:, :half])
        if low_ref is not None:
            new += dot(old, low_ref[...])
        new = new.astype(BF)
        pair_ref[rows_of(t), :half] = new
        kk_ref[...] += dot_tn(new, new)
        return carry

    def square_moving(t, carry):
        block = moving[rows_of(t), :]
        mm_ref[...] += dot_tn(block, block)
        return carry

    def leave(t, carry):
        swap(t).start()
        return carry

    lax.fori_loop(0, tiles, turn_kept, 0)
    if not first:
        lax.fori_loop(0, tiles, square_moving, 0)
    pl.semaphore_wait(barrier, group)
    lax.fori_loop(0, tiles, leave, 0)
    if first:
        lax.fori_loop(0, tiles, square_moving, 0)
    shape = (group, rows_each, half + quarter)
    part_a[...] = jnp.concatenate(
        [packed(kk_ref[...]).reshape(shape), packed(mm_ref[...]).reshape(shape)], axis=1
    ).astype(BF)
    start_sum(part_a, landed_a, sems_a)

    hand = to((me_r, partner), gram_a.at[me_r], handed, hands.at[0], hands.at[1])

    def reduce_a():
        gram_a[me_r] = with_low_diagonals(end_sum(landed_a, sems_a))
        hand.start()

    def cross(t, carry):
        if bit:
            pl.when(t == tiles - 1)(reduce_a)
        swap(t).wait()
        km_ref[...] += dot_tn(pair_ref[rows_of(t), :half], pair_ref[rows_of(t), half:])
        return carry

    lax.fori_loop(0, tiles, cross, 0)
    part_b[...] = km_ref[...].reshape(group, half // group, half).astype(kind)
    start_sum(part_b, landed_b, sems_b)
    if not bit:
        reduce_a()
    hand.wait()
    own = gram_a[me_r].astype(F32)
    place = lax.broadcasted_iota(jnp.int32, own.shape, 0)
    gram_a[me_r] = jnp.where(place < rows_each, own, handed[...].astype(F32)).astype(BF)
    start_gather(gram_a, sems_a)
    gram_b[me_r] = end_sum(landed_b, sems_b).astype(kind)
    start_gather(gram_b, sems_b)
    wait_all(part_a, sems_a.at[0])
    wait_all(part_b, sems_b.at[0])
    wait_all(gram_a, sems_a.at[3])
    wait_all(gram_b, sems_b.at[3])
    wait_all(gram_a, sems_a.at[2])
    wait_all(gram_b, sems_b.at[2])


def meet(p, *rest, bit, first, site):
    rows, total = p.shape
    half, quarter = total // 2, total // 4
    group = lax.axis_size("rows")
    chunk = half // group
    kind = F32 if first else BF
    side = (group, chunk, half + quarter)
    side_low = (group, chunk, total)
    full = (group, chunk, half)
    place = pl.BlockSpec(memory_space=pl.ANY if first else pltpu.VMEM)
    scratch = [
        pltpu.VMEM(side, BF),
        pltpu.VMEM(side, BF),
        pltpu.VMEM(side_low[1:], BF),
        pltpu.VMEM(full, kind),
        pltpu.VMEM(full, kind),
        pltpu.VMEM((3, half, half), F32),
        pltpu.SemaphoreType.DMA((2, rows // TILE)),
        pltpu.SemaphoreType.DMA((2, 4)),
        pltpu.SemaphoreType.DMA((2,)),
    ]
    if first:
        scratch = [
            pltpu.VMEM((rows, total), BF),
            pltpu.VMEM((rows, half), BF),
            pltpu.VMEM((1, total), jnp.int32),
            pltpu.VMEM((total, total), BF),
            pltpu.SemaphoreType.DMA((2,)),
        ] + scratch
    return pl.pallas_call(
        functools.partial(meet_kernel, bit, first),
        out_shape=(
            jax.ShapeDtypeStruct((rows, total), BF),
            jax.ShapeDtypeStruct(side_low, BF),
            jax.ShapeDtypeStruct(full, kind),
        ),
        in_specs=[place] * (1 + len(rest)),
        out_specs=[pl.BlockSpec(memory_space=pltpu.VMEM)] * 3,
        scratch_shapes=scratch,
        compiler_params=pltpu.CompilerParams(
            collective_id=site, has_side_effects=True, vmem_limit_bytes=48 << 20
        ),
        name=f"meet_bit{bit}",
    )(p, *rest)


def turn_kernel(last, p_ref, gram_a, gram_b, *outs):
    rows, total = p_ref.shape
    half = total // 2
    quarter = half // 2
    group = gram_a.shape[0]
    each = quarter // group
    g = gram_a[...].astype(F32)
    eye = lax.broadcasted_iota(jnp.int32, (half, half), 0) == lax.broadcasted_iota(
        jnp.int32, (half, half), 1
    )

    def whole(part):
        part = part.reshape(quarter, -1)
        wide = half + quarter
        low = jnp.concatenate([part[:, wide : wide + 1], part[:, wide + 1 : wide + 2]], axis=0)
        return unpacked(part[:, :wide]) + jnp.where(eye, low, 0.0)

    kk, mm = whole(g[:, :each, :]), whole(g[:, each:, :])
    high, low = split(rotation(kk, gram_b[...].astype(F32).reshape(half, half), mm))
    if not last:
        high_ref, low_ref, moving = outs
        high_ref[...], low_ref[...] = high[:, :half], low[:, :half]
        for t in range(0, rows, TILE):
            tile = p_ref[t : t + TILE, :]
            moving[t : t + TILE, :] = (dot(tile, high[:, half:]) + dot(tile, low[:, half:])).astype(BF)
        return
    out_ref, tiles, sems = outs
    copies = []
    for t in range(rows // TILE):
        here = pl.ds(t * TILE, TILE)
        tile = p_ref[t * TILE : (t + 1) * TILE, :]
        tiles[t] = dot(tile, high) + dot(tile, low)
        copies.append(pltpu.make_async_copy(tiles.at[t], out_ref.at[here, :], sems.at[t]))
        copies[-1].start()
    for copy in copies:
        copy.wait()


def turn(p, gram_a, gram_b, last):
    rows, total = p.shape
    vmem = pl.BlockSpec(memory_space=pltpu.VMEM)
    if last:
        out = [jax.ShapeDtypeStruct((rows, total), F32)]
        scratch = [pltpu.VMEM((rows // TILE, TILE, total), F32)]
        scratch += [pltpu.SemaphoreType.DMA((rows // TILE,))]
    else:
        out = [jax.ShapeDtypeStruct((total, total // 2), BF)] * 2
        out, scratch = out + [jax.ShapeDtypeStruct((rows, total // 2), BF)], []
    return pl.pallas_call(
        functools.partial(turn_kernel, last),
        out_shape=out,
        in_specs=[vmem] * 3,
        out_specs=[pl.BlockSpec(memory_space=pl.ANY)] if last else [vmem] * 3,
        scratch_shapes=scratch,
        compiler_params=pltpu.CompilerParams(vmem_limit_bytes=48 << 20),
        name="last_turn" if last else "turn",
    )(p, gram_a, gram_b)


def shards(columns, column_order, section_bits):
    levels = lax.axis_size("cols").bit_length() - 1
    p, rest = columns, [column_order.reshape(1, -1)]
    for s in range(SECTIONS):
        branches = [
            functools.partial(meet, bit=bit, first=s == 0, site=s * levels + bit)
            for bit in range(levels)
        ]
        p, gram_a, gram_b = lax.switch(section_bits[s], branches, p, *rest)
        rest = turn(p, gram_a, gram_b, s + 1 == SECTIONS)
    return rest[0]


def solution(mesh):
    return jax.shard_map(
        shards,
        mesh=mesh,
        in_specs=(P("rows", "cols"), P(), P()),
        out_specs=P("rows", "cols"),
        check_vma=False,
    )
```

```python
import functools

import jax
import jax.numpy as jnp
from jax import lax
from jax.experimental import pallas as pl
from jax.experimental.pallas import tpu as pltpu
from jax.sharding import PartitionSpec as P

SECTIONS = 3
ITERS = 4
EPS = 1e-06
THETA = 4.0
MESH = pl.DeviceIdType.MESH
BF = jnp.bfloat16
F32 = jnp.float32
TILE = 256


def dot(a, b):
    return jnp.dot(a, b, preferred_element_type=F32)


def dot_tn(a, b):
    return lax.dot_general(a, b, (((0,), (0,)), ((), ())), preferred_element_type=F32)


def dot_nt(a, b):
    return lax.dot_general(a, b, (((1,), (1,)), ((), ())), preferred_element_type=F32)


def split(a):
    high = a.astype(BF)
    return high, (a - high.astype(F32)).astype(BF)


def packed(block):
    half = block.shape[0] // 2
    return jnp.concatenate([block[:half, :], block[half:, half:]], axis=1)


def unpacked(block):
    half = block.shape[0]
    a, b, d = block[:, :half], block[:, half : 2 * half], block[:, 2 * half :]
    return jnp.concatenate(
        [jnp.concatenate([a, b], axis=1), jnp.concatenate([b.T, d], axis=1)], axis=0
    )


def rotation(kk, km, mm):
    width = kk.shape[0]
    total = 2 * width
    row = lax.broadcasted_iota(jnp.int32, (width, width), 0)
    col = lax.broadcasted_iota(jnp.int32, (width, width), 1)
    eye = row == col
    gap = (row - col).astype(F32) * (THETA / total)

    def inverse_roots(block, axis):
        d = jnp.sum(jnp.where(eye, block, 0.0), axis=axis, keepdims=True)
        return 1.0 / jnp.sqrt(d + EPS)

    k_col, k_row = inverse_roots(kk, 1), inverse_roots(kk, 0)
    m_col, m_row = inverse_roots(mm, 1), inverse_roots(mm, 0)
    c_kk = gap * (kk * (k_col * k_row))
    c_mm = gap * (mm * (m_col * m_row))
    c_km = (gap - THETA * 0.5) * (km * (k_col * m_row))
    frob = jnp.sum(c_kk * c_kk) + 2.0 * jnp.sum(c_km * c_km) + jnp.sum(c_mm * c_mm)
    z = jnp.concatenate(
        [jnp.concatenate([c_kk, c_km], axis=1), jnp.concatenate([-c_km.T, c_mm], axis=1)],
        axis=0,
    )
    scale = 1.0 / jnp.sqrt(jnp.full((1, 1), 1.0, F32) + frob)
    for k in range(ITERS):
        zb = z.astype(BF)
        w = dot_nt(zb, zb)
        if k:
            w = w + (z + z.T)
        square = scale * scale
        b = 1.5 - 0.5 * square
        z = z - (0.5 * square / b) * (w + dot(zb, w.astype(BF)))
        scale = scale * b
    row = lax.broadcasted_iota(jnp.int32, (total, total), 0)
    col = lax.broadcasted_iota(jnp.int32, (total, total), 1)
    return scale * (z + jnp.where(row == col, 1.0, 0.0))


def meet_kernel(bit, first, p_ref, *rest):
    if first:
        order_hbm, pair_ref, gram_a, gram_b, old_ref, moving, order_ref, high_ref, load_sems, *rest = rest
        low_ref = None
    else:
        high_ref, low_ref, moving, pair_ref, gram_a, gram_b, *rest = rest
        old_ref = p_ref
    part_a, landed_a, handed, part_b, landed_b, g_ref, swap_sems, sums, hands = rest
    kind = part_b.dtype
    kk_ref, km_ref, mm_ref = g_ref.at[0], g_ref.at[1], g_ref.at[2]
    group = lax.axis_size("rows")
    ring = group // 2
    me_r, me_c = lax.axis_index("rows"), lax.axis_index("cols")
    me_z, me_x = me_r // 2, me_r % 2
    rows, total = p_ref.shape
    half = total // 2
    quarter = half // 2
    tiles = rows // TILE
    rows_each = quarter // group
    partner = me_c + (1 << bit) * (1 - 2 * ((me_c // (1 << bit)) % 2))
    sems_a, sems_b = sums.at[0], sums.at[1]

    def each_peer(act):
        def visit(i, carry):
            k = i // 2
            z = ring // 2 + ((k + 1) // 2) * (1 - 2 * (k % 2))
            act(((me_z + z) % ring) * 2 + (me_x + 1 + i) % 2)
            return carry

        lax.fori_loop(0, group - 1, visit, 0)

    def to(device, source, target, send_sem, recv_sem):
        return pltpu.make_async_remote_copy(
            src_ref=source,
            dst_ref=target,
            send_sem=send_sem,
            recv_sem=recv_sem,
            device_id=device,
            device_id_type=MESH,
        )

    def rows_of(t):
        return pl.ds(pl.multiple_of(t * TILE, TILE), TILE)

    def swap(t):
        return to(
            (me_r, partner),
            moving.at[rows_of(t), :],
            pair_ref.at[rows_of(t), half:],
            swap_sems.at[0, t],
            swap_sems.at[1, t],
        )

    def wait_all(buffer, sem):
        others = buffer.at[pl.ds(0, group - 1)]
        pltpu.make_async_copy(others, others, sem).wait()

    def start_sum(part, landed, sems):
        each_peer(
            lambda peer: to(
                (peer, me_c), part.at[peer], landed.at[me_r], sems.at[0], sems.at[1]
            ).start()
        )
        landed[me_r] = part[me_r]

    def end_sum(landed, sems):
        wait_all(landed, sems.at[1])
        out = landed[0].astype(F32)
        for k in range(1, group):
            out += landed[k].astype(F32)
        return out

    def start_gather(gram, sems):
        each_peer(
            lambda peer: to(
                (peer, me_c), gram.at[me_r], gram.at[me_r], sems.at[2], sems.at[3]
            ).start()
        )

    def with_low_diagonals(block):
        high, low = split(block)
        row = lax.broadcasted_iota(jnp.int32, block.shape, 0) % rows_each + me_r * rows_each
        col = lax.broadcasted_iota(jnp.int32, block.shape, 1)
        low = low.astype(F32)
        first_low = jnp.sum(jnp.where(col == row, low, 0.0), axis=1, keepdims=True)
        last_low = jnp.sum(jnp.where(col == row + half, low, 0.0), axis=1, keepdims=True)
        lane = lax.broadcasted_iota(jnp.int32, (block.shape[0], quarter), 1)
        lows = jnp.where(lane == 0, first_low, jnp.where(lane == 1, last_low, 0.0))
        return jnp.concatenate([high, lows.astype(BF)], axis=1)

    barrier = pltpu.get_barrier_semaphore()
    each_peer(
        lambda peer: pl.semaphore_signal(
            barrier, inc=1, device_id=(peer, me_c), device_id_type=MESH
        )
    )
    pl.semaphore_signal(barrier, inc=1, device_id=(me_r, partner), device_id_type=MESH)

    if first:
        load = pltpu.make_async_copy(p_ref, old_ref, load_sems.at[0])
        load.start()
        load_order = pltpu.make_async_copy(order_hbm, order_ref, load_sems.at[1])
        load_order.start()
        load_order.wait()
        old_place = lax.broadcasted_iota(jnp.int32, (total, total), 0)
        high_ref[...] = jnp.where(old_place == order_ref[...], 1.0, 0.0).astype(BF)
        load.wait()

        def order_moving(t, carry):
            moving[rows_of(t), :] = dot(old_ref[rows_of(t), :], high_ref[:, half:]).astype(BF)
            return carry

        lax.fori_loop(0, tiles, order_moving, 0)

    def turn_kept(t, carry):
        old = old_ref[rows_of(t), :]
        new = dot(old, high_ref[:, :half])
        if low_ref is not None:
            new += dot(old, low_ref[...])
        pair_ref[rows_of(t), :half] = new.astype(BF)
        return carry

    def square(t, carry):
        kept, leaving = pair_ref[rows_of(t), :half], moving[rows_of(t), :]
        kk_ref[...] += dot_tn(kept, kept)
        mm_ref[...] += dot_tn(leaving, leaving)
        return carry

    def leave(t, carry):
        swap(t).start()
        return carry

    def local():
        g_ref[...] = jnp.zeros_like(g_ref)
        lax.fori_loop(0, tiles, square, 0)

    slow = bit != 0
    if not (first and slow):
        lax.fori_loop(0, tiles, turn_kept, 0)
    if not slow:
        local()
    pl.semaphore_wait(barrier, group)
    lax.fori_loop(0, tiles, leave, 0)
    if first and slow:
        lax.fori_loop(0, tiles, turn_kept, 0)
    if slow:
        local()
    shape = (group, rows_each, half + quarter)
    part_a[...] = jnp.concatenate(
        [packed(kk_ref[...]).reshape(shape), packed(mm_ref[...]).reshape(shape)], axis=1
    ).astype(BF)
    start_sum(part_a, landed_a, sems_a)

    hand = to((me_r, partner), gram_a.at[me_r], handed, hands.at[0], hands.at[1])

    def reduce_a():
        gram_a[me_r] = with_low_diagonals(end_sum(landed_a, sems_a))
        hand.start()

    def cross(t, carry):
        if bit:
            pl.when(t == tiles - 1)(reduce_a)
        swap(t).wait()
        km_ref[...] += dot_tn(pair_ref[rows_of(t), :half], pair_ref[rows_of(t), half:])
        return carry

    lax.fori_loop(0, tiles, cross, 0)
    part_b[...] = km_ref[...].reshape(group, half // group, half).astype(kind)
    start_sum(part_b, landed_b, sems_b)
    if not bit:
        reduce_a()
    hand.wait()
    own = gram_a[me_r].astype(F32)
    place = lax.broadcasted_iota(jnp.int32, own.shape, 0)
    gram_a[me_r] = jnp.where(place < rows_each, own, handed[...].astype(F32)).astype(BF)
    start_gather(gram_a, sems_a)
    gram_b[me_r] = end_sum(landed_b, sems_b).astype(kind)
    start_gather(gram_b, sems_b)
    wait_all(part_a, sems_a.at[0])
    wait_all(part_b, sems_b.at[0])
    wait_all(gram_a, sems_a.at[3])
    wait_all(gram_b, sems_b.at[3])
    wait_all(gram_a, sems_a.at[2])
    wait_all(gram_b, sems_b.at[2])


def meet(p, *rest, bit, first, site):
    rows, total = p.shape
    half, quarter = total // 2, total // 4
    group = lax.axis_size("rows")
    chunk = half // group
    kind = F32 if first else BF
    side = (group, chunk, half + quarter)
    side_low = (group, chunk, total)
    full = (group, chunk, half)
    place = pl.BlockSpec(memory_space=pl.ANY if first else pltpu.VMEM)
    scratch = [
        pltpu.VMEM(side, BF),
        pltpu.VMEM(side, BF),
        pltpu.VMEM(side_low[1:], BF),
        pltpu.VMEM(full, kind),
        pltpu.VMEM(full, kind),
        pltpu.VMEM((3, half, half), F32),
        pltpu.SemaphoreType.DMA((2, rows // TILE)),
        pltpu.SemaphoreType.DMA((2, 4)),
        pltpu.SemaphoreType.DMA((2,)),
    ]
    if first:
        scratch = [
            pltpu.VMEM((rows, total), BF),
            pltpu.VMEM((rows, half), BF),
            pltpu.VMEM((1, total), jnp.int32),
            pltpu.VMEM((total, total), BF),
            pltpu.SemaphoreType.DMA((2,)),
        ] + scratch
    return pl.pallas_call(
        functools.partial(meet_kernel, bit, first),
        out_shape=(
            jax.ShapeDtypeStruct((rows, total), BF),
            jax.ShapeDtypeStruct(side_low, BF),
            jax.ShapeDtypeStruct(full, kind),
        ),
        in_specs=[place] * (1 + len(rest)),
        out_specs=[pl.BlockSpec(memory_space=pltpu.VMEM)] * 3,
        scratch_shapes=scratch,
        compiler_params=pltpu.CompilerParams(
            collective_id=site, has_side_effects=True, vmem_limit_bytes=48 << 20
        ),
        name=f"meet_bit{bit}",
    )(p, *rest)


def turn_kernel(last, p_ref, gram_a, gram_b, *outs):
    rows, total = p_ref.shape
    half = total // 2
    quarter = half // 2
    group = gram_a.shape[0]
    each = quarter // group
    g = gram_a[...].astype(F32)
    eye = lax.broadcasted_iota(jnp.int32, (half, half), 0) == lax.broadcasted_iota(
        jnp.int32, (half, half), 1
    )

    def whole(part):
        part = part.reshape(quarter, -1)
        wide = half + quarter
        low = jnp.concatenate([part[:, wide : wide + 1], part[:, wide + 1 : wide + 2]], axis=0)
        return unpacked(part[:, :wide]) + jnp.where(eye, low, 0.0)

    kk, mm = whole(g[:, :each, :]), whole(g[:, each:, :])
    high, low = split(rotation(kk, gram_b[...].astype(F32).reshape(half, half), mm))
    if not last:
        high_ref, low_ref, moving = outs
        high_ref[...], low_ref[...] = high[:, :half], low[:, :half]
        for t in range(0, rows, TILE):
            tile = p_ref[t : t + TILE, :]
            moving[t : t + TILE, :] = (dot(tile, high[:, half:]) + dot(tile, low[:, half:])).astype(BF)
        return
    out_ref, tiles, sems = outs
    copies = []
    for t in range(rows // TILE):
        here = pl.ds(t * TILE, TILE)
        tile = p_ref[t * TILE : (t + 1) * TILE, :]
        tiles[t] = dot(tile, high) + dot(tile, low)
        copies.append(pltpu.make_async_copy(tiles.at[t], out_ref.at[here, :], sems.at[t]))
        copies[-1].start()
    for copy in copies:
        copy.wait()


def turn(p, gram_a, gram_b, last):
    rows, total = p.shape
    vmem = pl.BlockSpec(memory_space=pltpu.VMEM)
    if last:
        out = [jax.ShapeDtypeStruct((rows, total), F32)]
        scratch = [pltpu.VMEM((rows // TILE, TILE, total), F32)]
        scratch += [pltpu.SemaphoreType.DMA((rows // TILE,))]
    else:
        out = [jax.ShapeDtypeStruct((total, total // 2), BF)] * 2
        out, scratch = out + [jax.ShapeDtypeStruct((rows, total // 2), BF)], []
    return pl.pallas_call(
        functools.partial(turn_kernel, last),
        out_shape=out,
        in_specs=[vmem] * 3,
        out_specs=[pl.BlockSpec(memory_space=pl.ANY)] if last else [vmem] * 3,
        scratch_shapes=scratch,
        compiler_params=pltpu.CompilerParams(vmem_limit_bytes=48 << 20),
        name="last_turn" if last else "turn",
    )(p, gram_a, gram_b)


def shards(columns, column_order, section_bits):
    levels = lax.axis_size("cols").bit_length() - 1
    p, rest = columns, [column_order.reshape(1, -1)]
    for s in range(SECTIONS):
        branches = [
            functools.partial(meet, bit=bit, first=s == 0, site=s * levels + bit)
            for bit in range(levels)
        ]
        p, gram_a, gram_b = lax.switch(section_bits[s], branches, p, *rest)
        rest = turn(p, gram_a, gram_b, s + 1 == SECTIONS)
    return rest[0]


def solution(mesh):
    return jax.shard_map(
        shards,
        mesh=mesh,
        in_specs=(P("rows", "cols"), P(), P()),
        out_specs=P("rows", "cols"),
        check_vma=False,
    )
```

```python
import functools

import jax
import jax.numpy as jnp
from jax import lax
from jax.experimental import pallas as pl
from jax.experimental.pallas import tpu as pltpu
from jax.sharding import PartitionSpec as P

SECTIONS = 3
ITERS = 4
EPS = 1e-06
THETA = 4.0
MESH = pl.DeviceIdType.MESH
BF = jnp.bfloat16
F32 = jnp.float32
TILE = 256


def dot(a, b):
    return jnp.dot(a, b, preferred_element_type=F32)


def dot_tn(a, b):
    return lax.dot_general(a, b, (((0,), (0,)), ((), ())), preferred_element_type=F32)


def dot_nt(a, b):
    return lax.dot_general(a, b, (((1,), (1,)), ((), ())), preferred_element_type=F32)


def split(a):
    high = a.astype(BF)
    return high, (a - high.astype(F32)).astype(BF)


def packed(block):
    half = block.shape[0] // 2
    return jnp.concatenate([block[:half, :], block[half:, half:]], axis=1)


def unpacked(block):
    half = block.shape[0]
    a, b, d = block[:, :half], block[:, half : 2 * half], block[:, 2 * half :]
    return jnp.concatenate(
        [jnp.concatenate([a, b], axis=1), jnp.concatenate([b.T, d], axis=1)], axis=0
    )


def rotation(kk, km, mm):
    width = kk.shape[0]
    total = 2 * width
    row = lax.broadcasted_iota(jnp.int32, (width, width), 0)
    col = lax.broadcasted_iota(jnp.int32, (width, width), 1)
    eye = row == col
    gap = (row - col).astype(F32) * (THETA / total)

    def inverse_roots(block, axis):
        d = jnp.sum(jnp.where(eye, block, 0.0), axis=axis, keepdims=True)
        return 1.0 / jnp.sqrt(d + EPS)

    k_col, k_row = inverse_roots(kk, 1), inverse_roots(kk, 0)
    m_col, m_row = inverse_roots(mm, 1), inverse_roots(mm, 0)
    c_kk = gap * (kk * (k_col * k_row))
    c_mm = gap * (mm * (m_col * m_row))
    c_km = (gap - THETA * 0.5) * (km * (k_col * m_row))
    frob = jnp.sum(c_kk * c_kk) + 2.0 * jnp.sum(c_km * c_km) + jnp.sum(c_mm * c_mm)
    z = jnp.concatenate(
        [jnp.concatenate([c_kk, c_km], axis=1), jnp.concatenate([-c_km.T, c_mm], axis=1)],
        axis=0,
    )
    scale = 1.0 / jnp.sqrt(jnp.full((1, 1), 1.0, F32) + frob)
    for k in range(ITERS):
        zb = z.astype(BF)
        w = dot_nt(zb, zb)
        if k:
            w = w + (z + zb.T.astype(F32))
        square = scale * scale
        b = 1.5 - 0.5 * square
        z = z - (0.5 * square / b) * (w + dot(zb, w.astype(BF)))
        scale = scale * b
    row = lax.broadcasted_iota(jnp.int32, (total, total), 0)
    col = lax.broadcasted_iota(jnp.int32, (total, total), 1)
    return scale * (z + jnp.where(row == col, 1.0, 0.0))


def meet_kernel(bit, first, p_ref, *rest):
    if first:
        order_hbm, pair_ref, gram_a, gram_b, old_ref, moving, order_ref, high_ref, load_sems, *rest = rest
        low_ref = None
    else:
        high_ref, low_ref, moving, pair_ref, gram_a, gram_b, *rest = rest
        old_ref = p_ref
    part_a, landed_a, handed, part_b, landed_b, g_ref, swap_sems, sums, hands = rest
    kind = part_b.dtype
    kk_ref, km_ref, mm_ref = g_ref.at[0], g_ref.at[1], g_ref.at[2]
    group = lax.axis_size("rows")
    ring = group // 2
    me_r, me_c = lax.axis_index("rows"), lax.axis_index("cols")
    me_z, me_x = me_r // 2, me_r % 2
    rows, total = p_ref.shape
    half = total // 2
    quarter = half // 2
    tiles = rows // TILE
    rows_each = quarter // group
    partner = me_c + (1 << bit) * (1 - 2 * ((me_c // (1 << bit)) % 2))
    sems_a, sems_b = sums.at[0], sums.at[1]

    def each_peer(act):
        def visit(i, carry):
            k = i // 2
            z = ring // 2 + ((k + 1) // 2) * (1 - 2 * (k % 2))
            act(((me_z + z) % ring) * 2 + (me_x + 1 + i) % 2)
            return carry

        lax.fori_loop(0, group - 1, visit, 0)

    def to(device, source, target, send_sem, recv_sem):
        return pltpu.make_async_remote_copy(
            src_ref=source,
            dst_ref=target,
            send_sem=send_sem,
            recv_sem=recv_sem,
            device_id=device,
            device_id_type=MESH,
        )

    def rows_of(t):
        return pl.ds(pl.multiple_of(t * TILE, TILE), TILE)

    def swap(t):
        return to(
            (me_r, partner),
            moving.at[rows_of(t), :],
            pair_ref.at[rows_of(t), half:],
            swap_sems.at[0, t],
            swap_sems.at[1, t],
        )

    def wait_all(buffer, sem):
        others = buffer.at[pl.ds(0, group - 1)]
        pltpu.make_async_copy(others, others, sem).wait()

    def start_sum(part, landed, sems):
        each_peer(
            lambda peer: to(
                (peer, me_c), part.at[peer], landed.at[me_r], sems.at[0], sems.at[1]
            ).start()
        )
        landed[me_r] = part[me_r]

    def end_sum(landed, sems):
        wait_all(landed, sems.at[1])
        out = landed[0].astype(F32)
        for k in range(1, group):
            out += landed[k].astype(F32)
        return out

    def start_gather(gram, sems):
        each_peer(
            lambda peer: to(
                (peer, me_c), gram.at[me_r], gram.at[me_r], sems.at[2], sems.at[3]
            ).start()
        )

    def with_low_diagonals(block):
        high, low = split(block)
        row = lax.broadcasted_iota(jnp.int32, block.shape, 0) % rows_each + me_r * rows_each
        col = lax.broadcasted_iota(jnp.int32, block.shape, 1)
        low = low.astype(F32)
        first_low = jnp.sum(jnp.where(col == row, low, 0.0), axis=1, keepdims=True)
        last_low = jnp.sum(jnp.where(col == row + half, low, 0.0), axis=1, keepdims=True)
        lane = lax.broadcasted_iota(jnp.int32, (block.shape[0], quarter), 1)
        lows = jnp.where(lane == 0, first_low, jnp.where(lane == 1, last_low, 0.0))
        return jnp.concatenate([high, lows.astype(BF)], axis=1)

    barrier = pltpu.get_barrier_semaphore()
    each_peer(
        lambda peer: pl.semaphore_signal(
            barrier, inc=1, device_id=(peer, me_c), device_id_type=MESH
        )
    )
    pl.semaphore_signal(barrier, inc=1, device_id=(me_r, partner), device_id_type=MESH)

    if first:
        load = pltpu.make_async_copy(p_ref, old_ref, load_sems.at[0])
        load.start()
        load_order = pltpu.make_async_copy(order_hbm, order_ref, load_sems.at[1])
        load_order.start()
        load_order.wait()
        old_place = lax.broadcasted_iota(jnp.int32, (total, total), 0)
        high_ref[...] = jnp.where(old_place == order_ref[...], 1.0, 0.0).astype(BF)
        load.wait()

        def order_moving(t, carry):
            moving[rows_of(t), :] = dot(old_ref[rows_of(t), :], high_ref[:, half:]).astype(BF)
            return carry

        lax.fori_loop(0, tiles, order_moving, 0)

    def turn_kept(t, carry):
        old = old_ref[rows_of(t), :]
        new = dot(old, high_ref[:, :half])
        if low_ref is not None:
            new += dot(old, low_ref[...])
        pair_ref[rows_of(t), :half] = new.astype(BF)
        return carry

    def square(t, carry):
        kept, leaving = pair_ref[rows_of(t), :half], moving[rows_of(t), :]
        kk_ref[...] += dot_tn(kept, kept)
        mm_ref[...] += dot_tn(leaving, leaving)
        return carry

    def leave(t, carry):
        swap(t).start()
        return carry

    def local():
        g_ref[...] = jnp.zeros_like(g_ref)
        lax.fori_loop(0, tiles, square, 0)

    slow = bit != 0
    if not (first and slow):
        lax.fori_loop(0, tiles, turn_kept, 0)
    if not slow:
        local()
    pl.semaphore_wait(barrier, group)
    lax.fori_loop(0, tiles, leave, 0)
    if first and slow:
        lax.fori_loop(0, tiles, turn_kept, 0)
    if slow:
        local()
    shape = (group, rows_each, half + quarter)
    part_a[...] = jnp.concatenate(
        [packed(kk_ref[...]).reshape(shape), packed(mm_ref[...]).reshape(shape)], axis=1
    ).astype(BF)
    start_sum(part_a, landed_a, sems_a)

    hand = to((me_r, partner), gram_a.at[me_r], handed, hands.at[0], hands.at[1])

    def reduce_a():
        gram_a[me_r] = with_low_diagonals(end_sum(landed_a, sems_a))
        hand.start()

    def cross(t, carry):
        if bit:
            pl.when(t == tiles - 1)(reduce_a)
        swap(t).wait()
        km_ref[...] += dot_tn(pair_ref[rows_of(t), :half], pair_ref[rows_of(t), half:])
        return carry

    lax.fori_loop(0, tiles, cross, 0)
    part_b[...] = km_ref[...].reshape(group, half // group, half).astype(kind)
    start_sum(part_b, landed_b, sems_b)
    if not bit:
        reduce_a()
    hand.wait()
    own = gram_a[me_r].astype(F32)
    place = lax.broadcasted_iota(jnp.int32, own.shape, 0)
    gram_a[me_r] = jnp.where(place < rows_each, own, handed[...].astype(F32)).astype(BF)
    start_gather(gram_a, sems_a)
    gram_b[me_r] = end_sum(landed_b, sems_b).astype(kind)
    start_gather(gram_b, sems_b)
    wait_all(part_a, sems_a.at[0])
    wait_all(part_b, sems_b.at[0])
    wait_all(gram_a, sems_a.at[3])
    wait_all(gram_b, sems_b.at[3])
    wait_all(gram_a, sems_a.at[2])
    wait_all(gram_b, sems_b.at[2])


def meet(p, *rest, bit, first, site):
    rows, total = p.shape
    half, quarter = total // 2, total // 4
    group = lax.axis_size("rows")
    chunk = half // group
    kind = F32 if first else BF
    side = (group, chunk, half + quarter)
    side_low = (group, chunk, total)
    full = (group, chunk, half)
    place = pl.BlockSpec(memory_space=pl.ANY if first else pltpu.VMEM)
    scratch = [
        pltpu.VMEM(side, BF),
        pltpu.VMEM(side, BF),
        pltpu.VMEM(side_low[1:], BF),
        pltpu.VMEM(full, kind),
        pltpu.VMEM(full, kind),
        pltpu.VMEM((3, half, half), F32),
        pltpu.SemaphoreType.DMA((2, rows // TILE)),
        pltpu.SemaphoreType.DMA((2, 4)),
        pltpu.SemaphoreType.DMA((2,)),
    ]
    if first:
        scratch = [
            pltpu.VMEM((rows, total), BF),
            pltpu.VMEM((rows, half), BF),
            pltpu.VMEM((1, total), jnp.int32),
            pltpu.VMEM((total, total), BF),
            pltpu.SemaphoreType.DMA((2,)),
        ] + scratch
    return pl.pallas_call(
        functools.partial(meet_kernel, bit, first),
        out_shape=(
            jax.ShapeDtypeStruct((rows, total), BF),
            jax.ShapeDtypeStruct(side_low, BF),
            jax.ShapeDtypeStruct(full, kind),
        ),
        in_specs=[place] * (1 + len(rest)),
        out_specs=[pl.BlockSpec(memory_space=pltpu.VMEM)] * 3,
        scratch_shapes=scratch,
        compiler_params=pltpu.CompilerParams(
            collective_id=site, has_side_effects=True, vmem_limit_bytes=48 << 20
        ),
        name=f"meet_bit{bit}",
    )(p, *rest)


def turn_kernel(last, p_ref, gram_a, gram_b, *outs):
    rows, total = p_ref.shape
    half = total // 2
    quarter = half // 2
    group = gram_a.shape[0]
    each = quarter // group
    g = gram_a[...].astype(F32)
    eye = lax.broadcasted_iota(jnp.int32, (half, half), 0) == lax.broadcasted_iota(
        jnp.int32, (half, half), 1
    )

    def whole(part):
        part = part.reshape(quarter, -1)
        wide = half + quarter
        low = jnp.concatenate([part[:, wide : wide + 1], part[:, wide + 1 : wide + 2]], axis=0)
        return unpacked(part[:, :wide]) + jnp.where(eye, low, 0.0)

    kk, mm = whole(g[:, :each, :]), whole(g[:, each:, :])
    high, low = split(rotation(kk, gram_b[...].astype(F32).reshape(half, half), mm))
    if not last:
        high_ref, low_ref, moving = outs
        high_ref[...], low_ref[...] = high[:, :half], low[:, :half]
        for t in range(0, rows, TILE):
            tile = p_ref[t : t + TILE, :]
            moving[t : t + TILE, :] = (dot(tile, high[:, half:]) + dot(tile, low[:, half:])).astype(BF)
        return
    out_ref, tiles, sems = outs
    copies = []
    for t in range(rows // TILE):
        here = pl.ds(t * TILE, TILE)
        tile = p_ref[t * TILE : (t + 1) * TILE, :]
        tiles[t] = dot(tile, high) + dot(tile, low)
        copies.append(pltpu.make_async_copy(tiles.at[t], out_ref.at[here, :], sems.at[t]))
        copies[-1].start()
    for copy in copies:
        copy.wait()


def turn(p, gram_a, gram_b, last):
    rows, total = p.shape
    vmem = pl.BlockSpec(memory_space=pltpu.VMEM)
    if last:
        out = [jax.ShapeDtypeStruct((rows, total), F32)]
        scratch = [pltpu.VMEM((rows // TILE, TILE, total), F32)]
        scratch += [pltpu.SemaphoreType.DMA((rows // TILE,))]
    else:
        out = [jax.ShapeDtypeStruct((total, total // 2), BF)] * 2
        out, scratch = out + [jax.ShapeDtypeStruct((rows, total // 2), BF)], []
    return pl.pallas_call(
        functools.partial(turn_kernel, last),
        out_shape=out,
        in_specs=[vmem] * 3,
        out_specs=[pl.BlockSpec(memory_space=pl.ANY)] if last else [vmem] * 3,
        scratch_shapes=scratch,
        compiler_params=pltpu.CompilerParams(vmem_limit_bytes=48 << 20),
        name="last_turn" if last else "turn",
    )(p, gram_a, gram_b)


def shards(columns, column_order, section_bits):
    levels = lax.axis_size("cols").bit_length() - 1
    p, rest = columns, [column_order.reshape(1, -1)]
    for s in range(SECTIONS):
        branches = [
            functools.partial(meet, bit=bit, first=s == 0, site=s * levels + bit)
            for bit in range(levels)
        ]
        p, gram_a, gram_b = lax.switch(section_bits[s], branches, p, *rest)
        rest = turn(p, gram_a, gram_b, s + 1 == SECTIONS)
    return rest[0]


def solution(mesh):
    return jax.shard_map(
        shards,
        mesh=mesh,
        in_specs=(P("rows", "cols"), P(), P()),
        out_specs=P("rows", "cols"),
        check_vma=False,
    )
```
